512 devices in a mesh: aa: 16 (over z_hi, y), ba: 4 (over x), col: 8 (over z_lo, core).
Axes of the slice: x: 4, y: 4, z: 16 (z_hi: 4, z_lo: 4; z = z_hi * 4 + z_lo), core: 2. Of those that a mesh axis runs over, the one named last changes fastest.
Arguments:
- field: float32 [512, 128, 4096], P('aa', 'ba', 'col'), may hold values from -85 to 85
- factor: float32 [512, 256], P('aa'), may hold values from -0.25 to 0.25
Outputs:
- gram: float32 [512, 512], P('aa')
- truncated: float32 [256, 128, 4096], P('aa', 'ba', 'col')
The draws below stay inside these ranges and needn't reach their ends.
All inputs are finite; a program needn't handle non-finite values.
Results may differ from the reference program's by a relative error of at most 0.00011.
Values sent between devices are 32-bit elements; how exact they have to be, the bound alone decides.
No kernel may reach another device: no remote copies, remote signals or barrier semaphores. Data moves between devices by JAX's collectives and lax.ppermute only.
A program may use at most 64 MiB of HBM per device.

```python
import math
import jax
import jax.numpy as jnp
from jax import lax

I1 = 512
R = 256
F = 32
I2 = 128
I3 = 128
COLS = 4096


def draw_field(key, part):
    key = jax.random.fold_in(key, 1)
    key_rows, key_noise, key_weight, key_shared = jax.random.split(key, 4)
    scales = jnp.exp(jax.random.uniform(key_rows, (I1, 1, 1), jnp.float32, 0.0, math.log(10.0)))
    noise = jnp.clip(jax.random.normal(key_noise, (I1, I2, COLS), jnp.float32), -4.0, 4.0)
    weights = jax.random.uniform(key_weight, (I1, 1, F), jnp.float32, 0.3, 1.0)
    tiled = jnp.tile(weights, (1, 1, I3))
    shared = jnp.clip(jax.random.normal(key_shared, (1, I2, COLS), jnp.float32), -3.0, 3.0)
    return (scales * (noise + tiled * shared)).astype(jnp.float32)


def steps_of(own_key, extent, cuts, low, high):
    loudness, own = 1.0, jax.random.fold_in(own_key, 6)
    for dim, parts in cuts:
        heights = jnp.exp(jax.random.uniform(jax.random.fold_in(own, dim), (parts,), jnp.float32, low / len(cuts), high / len(cuts)))
        loudness = loudness * jnp.repeat(heights, extent[dim] // parts).reshape([-1 if axis == dim else 1 for axis in range(len(extent))])
    return loudness


def bell_draw(rng, extent, scale, limit, shards=(), held_as=jnp.bfloat16):
    array = jax.random.normal(rng, extent, jnp.float32) * scale
    if len(shards) > 0:
        array = steps_of(rng, extent, shards, -0.22, 0.18) * array
    return jnp.clip(array, min=-limit, max=limit).astype(held_as)


def setup_inputs(seed: int = 0) -> dict:
    keys = jax.random.split(jax.random.key(seed), 3)
    return {
        "field": draw_field(jax.random.fold_in(keys[2], 71), 0),
        "factor": bell_draw(keys[1], (I1, R), I1 ** -0.5, 0.25, ((0, 16),), jnp.float32),
    }


def reference(field, factor):
    unfolding = field.reshape(I1, I2 * COLS)
    gram = jnp.dot(unfolding, unfolding.T, precision=lax.Precision.HIGHEST, preferred_element_type=jnp.float32)
    truncated = jnp.dot(factor.T, unfolding, precision=lax.Precision.HIGHEST, preferred_element_type=jnp.float32)
    return gram, truncated.reshape(R, I2, COLS)
```

```python
import jax
import jax.numpy as jnp
from jax import lax
from jax.sharding import Mesh, PartitionSpec as P

AXES = ("zh", "y", "x", "zl", "core")
FIBRE = ("zh", "y")
PRECISION = lax.Precision.HIGH


def exchange(value, axis):
    return lax.all_to_all(value, axis, split_axis=0, concat_axis=0, tiled=True)


def swap(value, axis, flip):
    count = 2 if axis == "core" else 4
    return lax.ppermute(value, axis, [(i, i ^ flip) for i in range(count)])


def pick(value, index):
    return lax.dynamic_index_in_dim(value, index, 0, keepdims=False)


def scatter_sum(value, axis):
    own = lax.axis_index(axis)
    came = swap(jnp.stack([pick(value, own ^ 1), pick(value, own ^ 2)]), axis, 1)
    across = pick(value, own ^ 3) + came[1]
    return pick(value, own) + came[0] + swap(across, axis, 3)


def gather(value, axis):
    own = lax.axis_index(axis)
    pair = jnp.stack([value, swap(value, axis, 1)])
    far = swap(pair, axis, 3)
    by_flip = jnp.concatenate([pair, far[::-1]])
    return jnp.stack([pick(by_flip, own ^ j) for j in range(4)])


def gather_factor(factor):
    rows, kept = factor.shape
    part = lax.dynamic_slice_in_dim(factor, lax.axis_index("x") * (rows // 4), rows // 4, 0)
    return gather(part, "zh")


def spread_factor(parts):
    parts = gather(gather(parts, "y"), "x")
    return parts.transpose(2, 1, 0, 3, 4).reshape(-1, parts.shape[-1])


def reduce_gram(partial_gram):
    order = partial_gram.shape[0]
    half = order // 2
    core = lax.axis_index("core")
    other = lax.dynamic_slice_in_dim(partial_gram, (1 - core) * half, half, 1)
    own = lax.dynamic_slice_in_dim(partial_gram, core * half, half, 1)
    terms = (own + swap(other, "core", 1)).reshape(4, 4, order // 16, half)
    terms = scatter_sum(terms.transpose(1, 0, 2, 3), "y")
    rows = scatter_sum(terms, "zh")
    rows = rows + swap(rows, "zl", 1)
    rows = rows + swap(rows, "zl", 2)
    rows = rows + swap(rows, "x", 1)
    rows = rows + swap(rows, "x", 3)
    beside = swap(rows, "core", 1)
    return jnp.concatenate([jnp.where(core == 0, rows, beside), jnp.where(core == 0, beside, rows)], axis=1)


def body(field, factor):
    rows, cells, columns = field.shape
    blocks = field.reshape(rows, 16, cells * columns // 16).transpose(1, 0, 2)
    blocks, parts = lax.optimization_barrier((blocks, gather_factor(factor)))
    fibres = exchange(blocks, FIBRE).reshape(rows * 16, -1)
    whole_factor = spread_factor(parts)
    partial_gram = jnp.dot(fibres, fibres.T, precision=PRECISION, preferred_element_type=jnp.float32)
    cut = jnp.dot(whole_factor.T, fibres, precision=PRECISION, preferred_element_type=jnp.float32)
    back = exchange(cut.reshape(16, cut.shape[0] // 16, -1), FIBRE)
    gram = reduce_gram(partial_gram)
    truncated = back.transpose(1, 0, 2).reshape(back.shape[1], cells, columns)
    return gram, truncated


def solution(mesh):
    fine = Mesh(mesh.devices.reshape(4, 4, 4, 4, 2), AXES)
    last = ("zl", "core")
    return jax.shard_map(
        body,
        mesh=fine,
        in_specs=(P(FIBRE, "x", last), P(FIBRE, None)),
        out_specs=(P(FIBRE, None), P(FIBRE, "x", last)),
        check_vma=False,
    )
```

```python
import jax
import jax.numpy as jnp
from jax import lax
from jax.sharding import Mesh, PartitionSpec as P

AXES = ("zh", "y", "x", "zl", "core")
FIBRE = ("zh", "y")
PRECISION = lax.Precision.HIGH
F32 = jnp.float32


def exchange(value, axis):
    return lax.all_to_all(value, axis, split_axis=0, concat_axis=0, tiled=True)


def swap(value, axis, flip):
    count = 2 if axis == "core" else 4
    return lax.ppermute(value, axis, [(i, i ^ flip) for i in range(count)])


def pick(value, index):
    return lax.dynamic_index_in_dim(value, index, 0, keepdims=False)


def by_owner(by_flip, own):
    held = jnp.stack(by_flip)
    return jnp.stack([pick(held, own ^ j) for j in range(4)])


def sum_swapped(parts, axis):
    far = [swap(parts[k], axis, k) for k in (2, 1, 3)]
    return (parts[0] + far[1]) + (far[0] + far[2])


def scatter_sum(value, axis):
    own = lax.axis_index(axis)
    return sum_swapped([pick(value, own ^ k) for k in range(4)], axis)


def gather(value, axis):
    own = lax.axis_index(axis)
    pair = jnp.stack([value, swap(value, axis, 1)])
    far = swap(pair, axis, 3)
    return by_owner([pair[0], pair[1], far[1], far[0]], own)


def gather_zh(factor):
    rows = factor.shape[0] // 4
    part = lax.dynamic_slice_in_dim(factor, lax.axis_index("x") * rows, rows, 0)
    return [part] + [swap(part, "zh", k) for k in (1, 2, 3)]


def spread_factor(parts):
    parts = gather(gather(by_owner(parts, lax.axis_index("zh")), "y"), "x")
    return parts.transpose(2, 1, 0, 3, 4).reshape(-1, parts.shape[-1])


def reduce_gram(partial_gram):
    order = partial_gram.shape[0]
    half = order // 2
    core = lax.axis_index("core")
    other = lax.dynamic_slice_in_dim(partial_gram, (1 - core) * half, half, 1)
    own = lax.dynamic_slice_in_dim(partial_gram, core * half, half, 1)
    terms = (own + swap(other, "core", 1)).reshape(4, 4, order // 16, half)
    terms = scatter_sum(terms.transpose(1, 0, 2, 3), "y")
    terms = sum_swapped([terms] * 4, "x")
    rows = scatter_sum(terms, "zh")
    rows = rows + swap(rows, "zl", 1)
    rows = rows + swap(rows, "zl", 2)
    beside = swap(rows, "core", 1)
    return jnp.concatenate([jnp.where(core == 0, rows, beside), jnp.where(core == 0, beside, rows)], axis=1)


def dot(a, b):
    return jnp.dot(a, b, precision=PRECISION, preferred_element_type=F32)


def body(field, factor):
    rows, cells, columns = field.shape
    blocks = field.reshape(rows, 16, cells * columns // 16).transpose(1, 0, 2)
    blocks, parts = lax.optimization_barrier((blocks, gather_zh(factor)))
    fibres = exchange(blocks, FIBRE).reshape(rows * 16, -1)
    whole_factor = spread_factor(parts)
    cut = dot(whole_factor.T, fibres)
    kept = cut.shape[0] // 16
    back = exchange(cut.reshape(16, kept, -1), FIBRE)
    gram = reduce_gram(dot(fibres, fibres.T))
    return gram, back.transpose(1, 0, 2).reshape(kept, cells, columns)


def solution(mesh):
    fine = Mesh(mesh.devices.reshape(4, 4, 4, 4, 2), AXES)
    last = ("zl", "core")
    return jax.shard_map(
        body,
        mesh=fine,
        in_specs=(P(FIBRE, "x", last), P(FIBRE, None)),
        out_specs=(P(FIBRE, None), P(FIBRE, "x", last)),
        check_vma=False,
    )
```

```python
import jax
import jax.numpy as jnp
from jax import lax
from jax.sharding import Mesh, PartitionSpec as P

AXES = ("zh", "y", "x", "zl", "core")
FIBRE = ("zh", "y")
PRECISION = lax.Precision.HIGH
F32 = jnp.float32


def exchange(value, axis):
    return lax.all_to_all(value, axis, split_axis=0, concat_axis=0, tiled=True)


def swap(value, axis, flip):
    count = 2 if axis == "core" else 4
    return lax.ppermute(value, axis, [(i, i ^ flip) for i in range(count)])


def pick(value, index):
    return lax.dynamic_index_in_dim(value, index, 0, keepdims=False)


def by_owner(by_flip, own):
    held = jnp.stack(by_flip)
    return jnp.stack([pick(held, own ^ j) for j in range(4)])


def sum_swapped(parts, axis):
    far = [swap(parts[k], axis, k) for k in (2, 1, 3)]
    return (parts[0] + far[1]) + (far[0] + far[2])


def scatter_sum(value, axis):
    own = lax.axis_index(axis)
    return sum_swapped([pick(value, own ^ k) for k in range(4)], axis)


def gather(value, axis):
    own = lax.axis_index(axis)
    pair = jnp.stack([value, swap(value, axis, 1)])
    far = swap(pair, axis, 3)
    return by_owner([pair[0], pair[1], far[1], far[0]], own)


def gather_zh(factor):
    rows = factor.shape[0] // 4
    part = lax.dynamic_slice_in_dim(factor, lax.axis_index("x") * rows, rows, 0)
    return lax.all_gather(part, "zh")


def spread_factor(parts):
    parts = gather(gather(parts, "y"), "x")
    return parts.transpose(2, 1, 0, 3, 4).reshape(-1, parts.shape[-1])


def reduce_gram(partial_gram):
    order = partial_gram.shape[0]
    half = order // 2
    core = lax.axis_index("core")
    other = lax.dynamic_slice_in_dim(partial_gram, (1 - core) * half, half, 1)
    own = lax.dynamic_slice_in_dim(partial_gram, core * half, half, 1)
    terms = (own + swap(other, "core", 1)).reshape(4, 4, order // 16, half)
    terms = scatter_sum(terms.transpose(1, 0, 2, 3), "y")
    terms = sum_swapped([terms] * 4, "x")
    rows = scatter_sum(terms, "zh")
    rows = rows + swap(rows, "zl", 1)
    rows = rows + swap(rows, "zl", 2)
    beside = swap(rows, "core", 1)
    return jnp.concatenate([jnp.where(core == 0, rows, beside), jnp.where(core == 0, beside, rows)], axis=1)


def dot(a, b):
    return jnp.dot(a, b, precision=PRECISION, preferred_element_type=F32)


def body(field, factor):
    rows, cells, columns = field.shape
    blocks = field.reshape(rows, 16, cells * columns // 16).transpose(1, 0, 2)
    blocks, parts = lax.optimization_barrier((blocks, gather_zh(factor)))
    fibres = exchange(blocks, FIBRE).reshape(rows * 16, -1)
    whole_factor = spread_factor(parts)
    cut = dot(whole_factor.T, fibres)
    kept = cut.shape[0] // 16
    back = exchange(cut.reshape(16, kept, -1), FIBRE)
    gram = reduce_gram(dot(fibres, fibres.T))
    return gram, back.transpose(1, 0, 2).reshape(kept, cells, columns)


def solution(mesh):
    fine = Mesh(mesh.devices.reshape(4, 4, 4, 4, 2), AXES)
    last = ("zl", "core")
    return jax.shard_map(
        body,
        mesh=fine,
        in_specs=(P(FIBRE, "x", last), P(FIBRE, None)),
        out_specs=(P(FIBRE, None), P(FIBRE, "x", last)),
        check_vma=False,
    )
```

```python
import jax
import jax.numpy as jnp
from jax import lax
from jax.sharding import Mesh, PartitionSpec as P

AXES = ("zh", "y", "x", "zl", "core")
FIBRE = ("zh", "y")
PRECISION = lax.Precision.HIGH
F32 = jnp.float32


def exchange(value, axis):
    return lax.all_to_all(value, axis, split_axis=0, concat_axis=0, tiled=True)


def swap(value, axis, flip):
    count = 2 if axis == "core" else 4
    return lax.ppermute(value, axis, [(i, i ^ flip) for i in range(count)])


def pick(value, index):
    return lax.dynamic_index_in_dim(value, index, 0, keepdims=False)


def by_owner(by_flip, own):
    held = jnp.stack(by_flip)
    return jnp.stack([pick(held, own ^ j) for j in range(4)])


def sum_swapped(parts, axis):
    far = [swap(parts[k], axis, k) for k in (2, 1, 3)]
    return (parts[0] + far[1]) + (far[0] + far[2])


def scatter_sum(value, axis):
    own = lax.axis_index(axis)
    return sum_swapped([pick(value, own ^ k) for k in range(4)], axis)


def gather(value, axis):
    own = lax.axis_index(axis)
    pair = jnp.stack([value, swap(value, axis, 1)])
    far = swap(pair, axis, 3)
    return by_owner([pair[0], pair[1], far[1], far[0]], own)


def gather_zh(factor):
    rows = factor.shape[0] // 4
    part = lax.dynamic_slice_in_dim(factor, lax.axis_index("x") * rows, rows, 0)
    return lax.all_gather(part, "zh")


def spread_factor(parts):
    parts = gather(gather(parts, "y"), "x")
    return parts.transpose(2, 1, 0, 3, 4).reshape(-1, parts.shape[-1])


def reduce_gram(partial_gram):
    order = partial_gram.shape[0]
    half = order // 2
    core = lax.axis_index("core")
    other = lax.dynamic_slice_in_dim(partial_gram, (1 - core) * half, half, 1)
    own = lax.dynamic_slice_in_dim(partial_gram, core * half, half, 1)
    terms = (own + swap(other, "core", 1)).reshape(4, 4, order // 16, half)
    terms = scatter_sum(terms.transpose(1, 0, 2, 3), "y")
    terms = lax.all_gather(terms, "x").sum(0)
    rows = scatter_sum(terms, "zh")
    rows = rows + swap(rows, "zl", 1)
    rows = rows + swap(rows, "zl", 2)
    return lax.all_gather(rows, "core", axis=1, tiled=True)


def dot(a, b):
    return jnp.dot(a, b, precision=PRECISION, preferred_element_type=F32)


def body(field, factor):
    rows, cells, columns = field.shape
    blocks = field.reshape(rows, 16, cells * columns // 16).transpose(1, 0, 2)
    blocks, parts = lax.optimization_barrier((blocks, gather_zh(factor)))
    fibres = exchange(blocks, FIBRE).reshape(rows * 16, -1)
    whole_factor = spread_factor(parts)
    cut = dot(whole_factor.T, fibres)
    kept = cut.shape[0] // 16
    back = exchange(cut.reshape(16, kept, -1), FIBRE)
    gram = reduce_gram(dot(fibres, fibres.T))
    return gram, back.transpose(1, 0, 2).reshape(kept, cells, columns)


def solution(mesh):
    fine = Mesh(mesh.devices.reshape(4, 4, 4, 4, 2), AXES)
    last = ("zl", "core")
    return jax.shard_map(
        body,
        mesh=fine,
        in_specs=(P(FIBRE, "x", last), P(FIBRE, None)),
        out_specs=(P(FIBRE, None), P(FIBRE, "x", last)),
        check_vma=False,
    )
```

```python
import jax
import jax.numpy as jnp
from jax import lax
from jax.sharding import Mesh, PartitionSpec as P

AXES = ("zh", "y", "x", "zl", "core")
FIBRE = ("zh", "y")
PRECISION = lax.Precision.HIGH
F32 = jnp.float32


def exchange(value, axis):
    return lax.all_to_all(value, axis, split_axis=0, concat_axis=0, tiled=True)


def swap(value, axis, flip):
    count = 2 if axis == "core" else 4
    return lax.ppermute(value, axis, [(i, i ^ flip) for i in range(count)])


def pick(value, index):
    return lax.dynamic_index_in_dim(value, index, 0, keepdims=False)


def by_owner(by_flip, own):
    held = jnp.stack(by_flip)
    return jnp.stack([pick(held, own ^ j) for j in range(4)])


def sum_swapped(parts, axis):
    far = [swap(parts[k], axis, k) for k in (2, 1, 3)]
    return (parts[0] + far[1]) + (far[0] + far[2])


def scatter_sum(value, axis):
    own = lax.axis_index(axis)
    return sum_swapped([pick(value, own ^ k) for k in range(4)], axis)


def gather(value, axis):
    own = lax.axis_index(axis)
    pair = jnp.stack([value, swap(value, axis, 1)])
    far = swap(pair, axis, 3)
    return by_owner([pair[0], pair[1], far[1], far[0]], own)


def gather_zh(factor):
    rows = factor.shape[0] // 4
    part = lax.dynamic_slice_in_dim(factor, lax.axis_index("x") * rows, rows, 0)
    return lax.all_gather(part, "zh")


def spread_factor(parts):
    parts = gather(gather(parts, "y"), "x")
    return parts.transpose(2, 1, 0, 3, 4).reshape(-1, parts.shape[-1])


def reduce_gram(partial_gram):
    order = partial_gram.shape[0]
    half = order // 2
    core = lax.axis_index("core")
    other = lax.dynamic_slice_in_dim(partial_gram, (1 - core) * half, half, 1)
    own = lax.dynamic_slice_in_dim(partial_gram, core * half, half, 1)
    terms = (own + swap(other, "core", 1)).reshape(4, 4, order // 16, half)
    terms = scatter_sum(terms.transpose(1, 0, 2, 3), "y")
    terms = lax.all_gather(terms, "x").sum(0)
    rows = scatter_sum(terms, "zh")
    shares = lax.all_gather(rows, ("zl", "core")).reshape(4, 2, *rows.shape).sum(0)
    return shares.transpose(1, 0, 2).reshape(rows.shape[0], order)


def dot(a, b):
    return jnp.dot(a, b, precision=PRECISION, preferred_element_type=F32)


def body(field, factor):
    rows, cells, columns = field.shape
    blocks = field.reshape(rows, 16, cells * columns // 16).transpose(1, 0, 2)
    blocks, parts = lax.optimization_barrier((blocks, gather_zh(factor)))
    fibres = exchange(blocks, FIBRE).reshape(rows * 16, -1)
    whole_factor = spread_factor(parts)
    cut = dot(whole_factor.T, fibres)
    kept = cut.shape[0] // 16
    back = exchange(cut.reshape(16, kept, -1), FIBRE)
    gram = reduce_gram(dot(fibres, fibres.T))
    return gram, back.transpose(1, 0, 2).reshape(kept, cells, columns)


def solution(mesh):
    fine = Mesh(mesh.devices.reshape(4, 4, 4, 4, 2), AXES)
    last = ("zl", "core")
    return jax.shard_map(
        body,
        mesh=fine,
        in_specs=(P(FIBRE, "x", last), P(FIBRE, None)),
        out_specs=(P(FIBRE, None), P(FIBRE, "x", last)),
        check_vma=False,
    )
```
